32 devices in a mesh: groups: 2 (over x), row: 16 (over z, y, core).
Axes of the slice: x: 2, y: 2, z: 4, core: 2. Of those that a mesh axis runs over, the one named last changes fastest.
Arguments:
- panels: bfloat16 [512, 8, 256], P(('groups', 'row')), parts along dimension 0, may hold values from -6 to 6
- diag_blocks: bfloat16 [512, 256, 256], P(('groups', 'row')), parts along dimension 0, may hold values from -0.1875 to 0.1875
- near_blocks: bfloat16 [512, 2, 256, 256], P(('groups', 'row')), parts along dimension 0, may hold values from -0.1875 to 0.1875
- near_offsets: int32 [512, 2], P(('groups', 'row')), parts along dimension 0, may hold values from 1 to 4
- far_u: bfloat16 [6144, 32, 256], P(('groups', 'row')), parts along dimension 0, may hold values from -0.375 to 0.375
- far_v: bfloat16 [6144, 32, 256], P(('groups', 'row')), parts along dimension 0, may hold values from -0.375 to 0.375
- far_row: int32 [6144], P(('groups', 'row')), parts along dimension 0, may hold values from 0 to 15
- far_owner: int32 [6144, 1], P(('groups', 'row')), parts along dimension 0, may hold values from 0 to 15; in each aligned block of 192 rows (0 to 191, 192 to 383, ...) at most 24 rows name the same one
- far_slot: int32 [6144], P(('groups', 'row')), parts along dimension 0, may hold values from 0 to 15
Outputs:
- product: float32 [512, 8, 256], P(('groups', 'row')), parts along dimension 0
The draws below stay inside these ranges and needn't reach their ends.
There are 2 independent parts, one for each index of `groups`. The reference program is written for one: setup_inputs(seed, part) draws one part's arguments, and reference() takes and returns one part's arrays. A program takes and returns all parts, laid end to end along the dimension named above; each array names one. Nothing has to cross between parts.
Inputs may be any that keep to these rules, and one draw needn't show every extreme that they name: `far_owner`: within the 192 rows of one device (aligned blocks of rows), no owner is named more than 24 times, a bound that some block reaches.
All inputs are finite; a program needn't handle non-finite values.
Results may differ from the reference program's by a relative error of at most 0.0025.
Values may be sent and summed in bfloat16 or wider, within the bound.
A program may use at most 128 MiB of HBM per device.

```python
import math
import jax
import jax.numpy as jnp
import numpy as np
from jax import lax

LEAF = 256
R = 32
NRHS = 8
LEAF_DEV = 16
NEAR_PER = 2
REACH = 4
LEAVES = 256
FAR_DEV = 192
FAR_PAIRS = 3072
CAP = 24
N_ROW = 16


def place_ends(values, key, low, top_value):
    longest = values.shape.index(max(values.shape))
    spots = []
    for shift in (0, 1):
        where = [jax.random.randint(jax.random.fold_in(key, axis), (), 0, length) for axis, length in enumerate(values.shape)]
        where[longest] = (where[longest] + shift) % values.shape[longest]
        spots.append(tuple(where))
    return values.at[spots[0]].set(low).at[spots[1]].set(top_value)


def shard_levels(key, dims, shards, least, largest):
    factor_of = 1.0
    for axis_at, parts in shards:
        steps = jax.random.uniform(jax.random.fold_in(jax.random.fold_in(key, 6), axis_at), (parts,), jnp.float32, least / len(shards), largest / len(shards))
        factor_of = factor_of * jnp.repeat(jnp.exp(steps), dims[axis_at] // parts).reshape((-1,) + (1,) * (len(dims) - 1 - axis_at))
    return factor_of


def routed_block(rng, own, number, rows, count, top, bound, slope):
    sequence = jax.random.permutation(rng, count)
    crowded, common = shares(count, rows * top, bound, slope, True), shares(count, rows * top, bound, slope, False)
    places = jnp.arange(count)

    def named(sizes, turn):
        used = int((sizes > 0).sum())
        fixed = max(1, used // 4)
        shifted = fixed + (places - fixed + turn * (used - fixed)) % max(1, count - fixed)
        return jnp.zeros((count,), jnp.int32).at[sequence[jnp.where(places < fixed, places, shifted)]].set(jnp.asarray(sizes, jnp.int32))

    sizes = jnp.where(number % 4 == 0, named(crowded, number // 4), named(common, number - number // 4 - 1))
    mixed = jax.random.permutation(jax.random.fold_in(own, 3), count)
    source_of, sink = mixed[0:count // 2 * 2:2], mixed[1:count // 2 * 2:2]
    margin = jnp.minimum(sizes[source_of] - 1, bound - sizes[sink]) // 2
    margin = jnp.where((source_of == sequence[0]) | (sink == sequence[0]) | (sizes[sink] == 0), 0, jnp.maximum(margin, 0))
    shifted = jax.random.randint(jax.random.fold_in(own, 4), (count // 2,), 0, 1 << 20) % (margin + 1)
    sizes = sizes.at[source_of].add(-shifted).at[sink].add(shifted)
    labels = jnp.searchsorted(jnp.cumsum(sizes), jnp.arange(rows * top), side="right").astype(jnp.int32)
    grid = labels.reshape(top, rows).T
    grid = grid[jax.random.permutation(jax.random.fold_in(own, 1), rows)]
    turn = jax.random.randint(jax.random.fold_in(own, 2), (rows, 1), 0, top)
    return jnp.take_along_axis(grid, (jnp.arange(top)[None, :] + turn) % top, axis=1)


def shares(number_of, total, limit, lean, full):
    weights = [(1 << 20) // math.isqrt(grade ** lean) + 1 for grade in range(1, number_of + 1)]
    largest = limit if full else min(limit, max(-(-total // number_of), total * weights[0] // sum(weights)))
    least = 1 if total - largest >= number_of - 1 else 0
    holding, rest = [largest] + [least] * (number_of - 1), total - largest - least * (number_of - 1)
    while rest > 0:
        free = [i for i in range(1, number_of) if holding[i] < largest] or [i for i in range(1, number_of) if holding[i] < limit]
        pool, remaining = sum([weights[i] for i in free]), rest
        for i in free:
            addition = min(limit - holding[i], max(1, remaining * weights[i] // pool), rest)
            holding[i] = holding[i] + addition
            rest = rest - addition
    return np.array(holding)


def gaussian(stream_key, dims, width, limit, split=(), kind=jnp.bfloat16):
    drawn = width * jax.random.normal(stream_key, dims, jnp.float32)
    if split:
        drawn = drawn * shard_levels(stream_key, dims, split, -0.22, 0.18)
    return jnp.clip(drawn, -limit, limit).astype(kind)


def setup_inputs(seed: int = 0, part: int = 0) -> dict:
    seeds = jax.random.split(jax.random.key(seed), 10)
    own_keys = jax.random.split(jax.random.fold_in(seeds[9], part), 10)
    panels = gaussian(own_keys[0], (LEAVES, NRHS, LEAF), 1.0, 6.0, ((0, 16),))
    diag_blocks = gaussian(own_keys[1], (LEAVES, LEAF, LEAF), (4 * LEAF) ** -0.5, 0.1875, ((0, 16),))
    near_blocks = gaussian(own_keys[2], (LEAVES, NEAR_PER, LEAF, LEAF), (4 * LEAF) ** -0.5, 0.1875, ((0, 16),))
    near_offsets = place_ends(jax.random.randint(own_keys[3], (LEAVES, NEAR_PER), 1, REACH + 1), jax.random.fold_in(own_keys[3], 1), 1, REACH).astype(jnp.int32)
    far_u = gaussian(own_keys[4], (FAR_PAIRS, R, LEAF), (8 * R) ** -0.5, 0.375, ((0, 16),))
    far_v = gaussian(own_keys[5], (FAR_PAIRS, R, LEAF), LEAF ** -0.5, 0.375, ((0, 16),))
    far_row = place_ends(jax.random.randint(own_keys[6], (FAR_PAIRS,), 0, LEAF_DEV), jax.random.fold_in(own_keys[6], 1), 0, LEAF_DEV - 1).astype(jnp.int32)
    far_owner_keys = jax.random.split(jax.random.fold_in(own_keys[7], 1), FAR_PAIRS // FAR_DEV)
    far_owner_turns = jax.random.permutation(jax.random.fold_in(own_keys[7], 3), FAR_PAIRS // FAR_DEV)
    far_owner = jax.vmap(lambda own, number: routed_block(jax.random.fold_in(own_keys[7], 2), own, number, FAR_DEV, N_ROW, 1, CAP, 2))(far_owner_keys, far_owner_turns).reshape((FAR_PAIRS, 1))
    far_slot = place_ends(jax.random.randint(own_keys[8], (FAR_PAIRS,), 0, LEAF_DEV), jax.random.fold_in(own_keys[8], 1), 0, LEAF_DEV - 1).astype(jnp.int32)
    return {"panels": panels, "diag_blocks": diag_blocks, "near_blocks": near_blocks, "near_offsets": near_offsets, "far_u": far_u, "far_v": far_v, "far_row": far_row, "far_owner": far_owner, "far_slot": far_slot}


def reference(panels, diag_blocks, near_blocks, near_offsets, far_u, far_v, far_row, far_owner, far_slot):
    values = panels.astype(jnp.float32)
    result = jnp.einsum('inl,ilm->inm', values, diag_blocks.astype(jnp.float32))
    leaf_ids = jnp.arange(LEAVES, dtype=jnp.int32)[:, None]
    target = leaf_ids + near_offsets.astype(jnp.int32)
    inside = target < LEAVES
    clipped = jnp.minimum(target, LEAVES - 1).astype(jnp.int32)
    near_x = jnp.where(inside[:, :, None, None], values[clipped], jnp.float32(0.0))
    blocks = near_blocks.astype(jnp.float32)
    result = result + jnp.einsum('iknl,ikml->inm', near_x, blocks)
    backward = jnp.einsum('inl,iklm->iknm', values, blocks)
    backward = jnp.where(inside[:, :, None, None], backward, jnp.float32(0.0))
    result = result.at[clipped.reshape(-1)].add(backward.reshape(-1, NRHS, LEAF))
    pair_ids = jnp.arange(FAR_PAIRS, dtype=jnp.int32)
    row_leaf = ((pair_ids // FAR_DEV) * LEAF_DEV + far_row).astype(jnp.int32)
    col_leaf = (far_owner[:, 0] * LEAF_DEV + far_slot).astype(jnp.int32)
    basis_u = far_u.astype(jnp.float32)
    basis_v = far_v.astype(jnp.float32)
    row_panels = values[row_leaf]
    col_panels = values[col_leaf]
    reduced = jnp.einsum('pnl,prl->pnr', col_panels, basis_v).astype(jnp.bfloat16)
    reduced = lax.optimization_barrier(reduced).astype(jnp.float32)
    forward = jnp.einsum('pnr,prl->pnl', reduced, basis_u)
    projected = jnp.einsum('pnl,prl->pnr', row_panels, basis_u).astype(jnp.bfloat16)
    projected = lax.optimization_barrier(projected).astype(jnp.float32)
    returned = jnp.einsum('pnr,prl->pnl', projected, basis_v)
    result = result.at[row_leaf].add(forward)
    result = result.at[col_leaf].add(returned)
    return result
```

```python
import functools

import jax
import jax.numpy as jnp
from jax import lax
from jax.experimental import pallas as pl
from jax.experimental.pallas import tpu as pltpu
from jax.sharding import PartitionSpec as P

REACH = 4
GROUP = 16
F32, BF16 = jnp.float32, jnp.bfloat16


def dot(a, b):
    return lax.dot_general(a, b, (((1,), (0,)), ((), ())), preferred_element_type=F32)


def dot_t(a, b):
    return lax.dot_general(a, b, (((1,), (1,)), ((), ())), preferred_element_type=F32)


def eye(count):
    return lax.broadcasted_iota(jnp.int32, (count, count), 0) == lax.broadcasted_iota(
        jnp.int32, (count, count), 1
    )


def to_column(row):
    return jnp.sum(jnp.where(eye(row.shape[1]), row, 0), axis=1, keepdims=True)


def to_row(column):
    return jnp.sum(jnp.where(eye(column.shape[0]), column, 0), axis=0, keepdims=True)


def hits_wide(column, count):
    shape = (column.shape[0], count)
    return (column == lax.broadcasted_iota(jnp.int32, shape, 1)).astype(F32).astype(BF16)


def hits_tall(row, count):
    shape = (count, row.shape[1])
    return (row == lax.broadcasted_iota(jnp.int32, shape, 0)).astype(F32).astype(BF16)


def split(value):
    high = value.astype(BF16)
    return high, (value - high.astype(F32)).astype(BF16)


def scatter_rows(places, value):
    high, low = split(value)
    return dot(places, high) + dot(places, low)


def far_pass(picked, first, second, terms):
    rhs, pairs, width = picked.shape
    rank = first.shape[1]
    rows, lanes = rhs * GROUP, GROUP * rank
    row_pair = lax.broadcasted_iota(jnp.int32, (rows, lanes), 0) % GROUP
    lane_pair = lax.broadcasted_iota(jnp.int32, (rows, lanes), 1) // rank
    block = (row_pair == lane_pair).astype(F32).astype(BF16)

    def step(t, carry):
        here = pl.ds(pl.multiple_of(t * GROUP, GROUP), GROUP)
        left = picked[:, here, :].reshape(rows, width)
        one = first[here].reshape(lanes, width)
        two = second[here].reshape(lanes, width)
        inner = dot_t(left, one).astype(BF16) * block
        terms[:, here, :] = dot(inner, two).reshape(rhs, GROUP, width)
        return carry

    lax.fori_loop(0, pairs // GROUP, step, 0, unroll=2)


def near_terms(i, leaf_x, near_x, diag, near, off, acc):
    x = leaf_x.astype(BF16)
    acc[i] += dot(x, diag[i])
    for k in range(near.shape[1]):
        acc[i] += dot_t(near_x(i + off[i, k]).astype(BF16), near[i, k])
        back = dot(x, near[i, k])
        for d in range(1, REACH + 1):
            acc[i + d] += jnp.where(off[i, k] == d, back, 0.0)


def kernel(
    panels, diag_h, near_h, off, u_h, v_h, far_row, far_owner, far_slot, everything,
    out, sums,
    u, v, diag, near, x32, acc, picked, terms, sems,
):
    loads = [
        pltpu.make_async_copy(a, b, sems.at[s])
        for s, (a, b) in enumerate(((u_h, u), (v_h, v), (near_h, near), (diag_h, diag)))
    ]
    for load in loads:
        load.start()
    leaves, rhs, width = panels.shape
    peers = everything.shape[0]
    me = lax.axis_index("row")
    final = me == peers - 1
    following = jnp.minimum(me + 1, peers - 1)
    acc[...] = jnp.zeros_like(acc)
    x32[:leaves] = panels[...].astype(F32)
    for n in range(rhs):
        ahead = everything[following, n].astype(F32)[:REACH]
        x32[leaves:, n, :] = jnp.where(final, 0.0, ahead)

    rows_wide = hits_wide(to_column(far_row[...]), leaves)
    for n in range(rhs):
        picked[n] = dot(rows_wide, x32[:leaves, n, :].astype(BF16)).astype(BF16)
    loads[0].wait()
    loads[1].wait()
    far_pass(picked, u, v, terms)
    ids = to_row(far_owner[...]) * leaves + far_slot[...]
    places = hits_tall(ids, peers * leaves)
    for n in range(rhs):
        sums[:, n] = scatter_rows(places, terms[n]).astype(BF16).reshape(peers, leaves, width)

    loads[2].wait()
    loads[3].wait()

    def step(i, carry):
        near_terms(i, x32[i], lambda j: x32[j], diag, near, off, acc)
        return carry

    lax.fori_loop(0, leaves, step, 0, unroll=2)
    for n in range(rhs):
        spill = jnp.where(final, 0.0, acc[leaves:, n, :])
        spill = jnp.concatenate([spill, jnp.zeros((leaves - REACH, width), F32)], axis=0)
        sums[following, n] = (sums[following, n].astype(F32) + spill).astype(BF16)

    ids_wide = hits_wide(far_owner[...] * leaves + to_column(far_slot[...]), peers * leaves)
    for n in range(rhs):
        table = everything[:, n].reshape(peers * leaves, width)
        picked[n] = dot(ids_wide, table).astype(BF16)
    far_pass(picked, v, u, terms)
    rows_tall = hits_tall(far_row[...], leaves)
    for n in range(rhs):
        out[:, n, :] = acc[:leaves, n, :] + scatter_rows(rows_tall, terms[n])


def local(panels, diag_blocks, near_blocks, near_offsets, far_u, far_v, far_row, far_owner, far_slot):
    leaves, rhs, width = panels.shape
    pairs = far_row.shape[0]
    peers = lax.axis_size("row")
    everything = lax.all_gather(jnp.swapaxes(panels, 0, 1), "row", axis=0)
    vmem, anywhere = (pl.BlockSpec(memory_space=m) for m in (pltpu.VMEM, pl.ANY))
    out, sums = pl.pallas_call(
        kernel,
        out_shape=(
            jax.ShapeDtypeStruct(panels.shape, F32),
            jax.ShapeDtypeStruct((peers, rhs, leaves, width), BF16),
        ),
        in_specs=[
            vmem, anywhere, anywhere, pl.BlockSpec(memory_space=pltpu.SMEM),
            anywhere, anywhere, vmem, vmem, vmem, vmem,
        ],
        out_specs=(vmem, vmem),
        scratch_shapes=[
            pltpu.VMEM(far_u.shape, BF16),
            pltpu.VMEM(far_v.shape, BF16),
            pltpu.VMEM(diag_blocks.shape, BF16),
            pltpu.VMEM(near_blocks.shape, BF16),
            pltpu.VMEM((leaves + REACH, rhs, width), F32),
            pltpu.VMEM((leaves + REACH, rhs, width), F32),
            pltpu.VMEM((rhs, pairs, width), BF16),
            pltpu.VMEM((rhs, pairs, width), F32),
            pltpu.SemaphoreType.DMA((4,)),
        ],
        compiler_params=pltpu.CompilerParams(vmem_limit_bytes=56 << 20),
    )(
        panels, diag_blocks, near_blocks, near_offsets, far_u, far_v,
        far_row.reshape(1, pairs), far_owner, far_slot.reshape(1, pairs), everything,
    )
    got = lax.all_to_all(sums, "row", split_axis=0, concat_axis=0, tiled=True)
    return out + jnp.swapaxes(jnp.sum(got.astype(F32), axis=0), 0, 1)


def solution(mesh):
    split_all = ("groups", "row")
    return jax.shard_map(
        local,
        mesh=mesh,
        in_specs=tuple(P(split_all) for _ in range(9)),
        out_specs=P(split_all),
        check_vma=False,
    )
```

```python
import functools

import jax
import jax.numpy as jnp
from jax import lax
from jax.experimental import pallas as pl
from jax.experimental.pallas import tpu as pltpu
from jax.sharding import PartitionSpec as P

REACH = 4
GROUP = 16
F32, BF16 = jnp.float32, jnp.bfloat16


def dot(a, b):
    return lax.dot_general(a, b, (((1,), (0,)), ((), ())), preferred_element_type=F32)


def dot_t(a, b):
    return lax.dot_general(a, b, (((1,), (1,)), ((), ())), preferred_element_type=F32)


def eye(count):
    return lax.broadcasted_iota(jnp.int32, (count, count), 0) == lax.broadcasted_iota(
        jnp.int32, (count, count), 1
    )


def to_column(row):
    return jnp.sum(jnp.where(eye(row.shape[1]), row, 0), axis=1, keepdims=True)


def to_row(column):
    return jnp.sum(jnp.where(eye(column.shape[0]), column, 0), axis=0, keepdims=True)


def hits_wide(column, count):
    shape = (column.shape[0], count)
    return (column == lax.broadcasted_iota(jnp.int32, shape, 1)).astype(F32).astype(BF16)


def hits_tall(row, count):
    shape = (count, row.shape[1])
    return (row == lax.broadcasted_iota(jnp.int32, shape, 0)).astype(F32).astype(BF16)


def split(value):
    high = value.astype(BF16)
    return high, (value - high.astype(F32)).astype(BF16)


def scatter_rows(places, value):
    high, low = split(value)
    return dot(places, high) + dot(places, low)


def far_pass(picked, first, second, terms, begin, end):
    rhs, pairs, width = picked.shape
    rank = first.shape[1]
    rows, lanes = rhs * GROUP, GROUP * rank
    row_pair = lax.broadcasted_iota(jnp.int32, (rows, lanes), 0) % GROUP
    lane_pair = lax.broadcasted_iota(jnp.int32, (rows, lanes), 1) // rank
    block = (row_pair == lane_pair).astype(F32).astype(BF16)

    def step(t, carry):
        here = pl.ds(pl.multiple_of(t * GROUP, GROUP), GROUP)
        left = picked[:, here, :].reshape(rows, width)
        one = first[here].reshape(lanes, width)
        two = second[here].reshape(lanes, width)
        inner = dot_t(left, one).astype(BF16) * block
        terms[:, here, :] = dot(inner, two).reshape(rhs, GROUP, width)
        return carry

    lax.fori_loop(begin, end, step, 0, unroll=2)


def near_terms(i, leaf_x, near_x, diag, near, off, acc):
    x = leaf_x.astype(BF16)
    acc[i] += dot(x, diag[i])
    for k in range(near.shape[1]):
        acc[i] += dot_t(near_x(i + off[i, k]).astype(BF16), near[i, k])
        back = dot(x, near[i, k])
        for d in range(1, REACH + 1):
            acc[i + d] += jnp.where(off[i, k] == d, back, 0.0)


def kernel(
    shape, panels, diag_h, near_h, off, u_h, v_h, far_row, far_owner, far_slot,
    out,
    u, v, diag, near, x32, acc, picked, terms, everything, sums,
    got_core, pass_y, got_y, pass_z, got_z, spill, got_spill,
    load_sem, send_z, recv_z, send_y, recv_y, send_c, recv_c,
    send_1, recv_1, send_2, recv_2, send_3, recv_3, send_4, recv_4,
):
    zs, ys = shape
    loads = [
        pltpu.make_async_copy(a, b, load_sem.at[s])
        for s, (a, b) in enumerate(((u_h, u), (v_h, v), (near_h, near), (diag_h, diag)))
    ]
    for load in loads:
        load.start()
    leaves, rhs, width = panels.shape
    peers = everything.shape[0]
    me = lax.axis_index("row")
    c = lax.rem(me, 2)
    y = lax.rem(me // 2, ys)
    z = me // (2 * ys)
    final = me == peers - 1
    following = lax.rem(me + 1, peers)
    preceding = lax.rem(me + peers - 1, peers)

    def spot(zz, yy, cc):
        return (zz * ys + yy) * 2 + cc

    def up(d):
        return lax.rem(z + d, zs)

    def down(d):
        return lax.rem(z + zs - d, zs)

    sibling = spot(z, y, 1 - c)
    beside = spot(z, 1 - y, c) if ys == 2 else None
    column = [spot(up(d), y, c) for d in range(1, zs)]
    greeted = [sibling] + ([beside] if ys == 2 else []) + column + [following, preceding]
    barrier = pltpu.get_barrier_semaphore()
    for peer in greeted:
        pl.semaphore_signal(
            barrier, inc=1, device_id={"row": peer}, device_id_type=pl.DeviceIdType.MESH
        )

    x32[:leaves] = panels[...].astype(F32)
    x32[leaves:] = jnp.zeros((REACH, rhs, width), F32)
    acc[...] = jnp.zeros_like(acc)
    for n in range(rhs):
        everything[me, n] = x32[:leaves, n, :].astype(BF16)
    pl.semaphore_wait(barrier, len(greeted))

    sent = []

    def send(source, target, send_sem, recv_sem, peer):
        copy = pltpu.make_async_remote_copy(
            src_ref=source, dst_ref=target, send_sem=send_sem, recv_sem=recv_sem,
            device_id={"row": peer}, device_id_type=pl.DeviceIdType.MESH,
        )
        copy.start()
        sent.append(copy)

    def arrived(target, send_sem, recv_sem, peer):
        pltpu.make_async_remote_copy(
            src_ref=target, dst_ref=target, send_sem=send_sem, recv_sem=recv_sem,
            device_id={"row": peer}, device_id_type=pl.DeviceIdType.MESH,
        ).wait_recv()

    def share(owner, peer, send_sem, recv_sem):
        send(everything.at[owner], everything.at[owner], send_sem, recv_sem, peer)

    def settled(owner, send_sem, recv_sem):
        arrived(everything.at[owner], send_sem, recv_sem, sibling)

    far_first = list(range(zs - 1, 0, -1))
    for d in far_first:
        share(me, column[d - 1], send_z.at[d], recv_z.at[d])
    if ys == 2:
        share(me, beside, send_y.at[0], recv_y.at[0])
    share(me, sibling, send_c.at[0, 0], recv_c.at[0, 0])

    rows_wide = hits_wide(to_column(far_row[...]), leaves)
    for n in range(rhs):
        picked[n] = dot(rows_wide, x32[:leaves, n, :].astype(BF16)).astype(BF16)
    loads[0].wait()
    loads[1].wait()
    groups = far_row.shape[1] // GROUP
    far_pass(picked, u, v, terms, 0, groups // 2)
    for d in range(1, zs):
        owner = spot(down(d), y, c)
        settled(owner, send_z.at[d], recv_z.at[d])
        if ys == 2:
            share(owner, beside, send_y.at[d], recv_y.at[d])
        share(owner, sibling, send_c.at[0, d], recv_c.at[0, d])
    far_pass(picked, u, v, terms, groups // 2, groups)
    ids = to_row(far_owner[...]) * leaves + far_slot[...]
    places = hits_tall(ids, peers * leaves)
    for n in range(rhs):
        sums[:, :, n] = scatter_rows(places, terms[n]).astype(BF16).reshape(
            peers // 2, 2, leaves, width
        )

    order = far_first + [0]
    for d in order:
        send(
            sums.at[pl.ds(up(d) * ys, ys), 1 - c], got_core.at[d],
            send_1.at[d], recv_1.at[d], sibling,
        )
    if ys == 2:
        for d in range(zs):
            owner = spot(down(d), 1 - y, c)
            settled(owner, send_y.at[d], recv_y.at[d])
            share(owner, sibling, send_c.at[1, d], recv_c.at[1, d])

    loads[2].wait()
    loads[3].wait()

    def step(i, carry):
        near_terms(i, x32[i], lambda j: x32[j], diag, near, off, acc)
        return carry

    def joined(d, yy):
        return sums[up(d) * ys + yy, c].astype(F32) + got_core[d, yy].astype(F32)

    lax.fori_loop(0, 2, step, 0, unroll=2)
    for d in order:
        arrived(got_core.at[d], send_1.at[d], recv_1.at[d], sibling)
        if ys == 2:
            pass_y[d] = joined(d, 1 - y).astype(BF16)
            send(pass_y.at[d], got_y.at[d], send_2.at[d], recv_2.at[d], beside)
    lax.fori_loop(2, 8, step, 0, unroll=2)

    def merged(d):
        value = joined(d, y)
        if ys == 2:
            arrived(got_y.at[d], send_2.at[d], recv_2.at[d], beside)
            value = value + got_y[d].astype(F32)
        return value

    for d in far_first:
        pass_z[d] = merged(d).astype(BF16)
        send(pass_z.at[d], got_z.at[d], send_3.at[d], recv_3.at[d], column[d - 1])
    lax.fori_loop(8, leaves - REACH, step, 0, unroll=2)

    for part in range(ys):
        for d in range(zs):
            owner = spot(down(d), y if part == 0 else 1 - y, 1 - c)
            settled(owner, send_c.at[part, d], recv_c.at[part, d])
    for n in range(rhs):
        ahead = everything[following, n].astype(F32)[:REACH]
        x32[leaves:, n, :] = jnp.where(final, 0.0, ahead)
    lax.fori_loop(leaves - REACH, leaves, step, 0, unroll=2)
    spill[...] = acc[leaves:]
    send(spill, got_spill, send_4, recv_4, following)

    ids_wide = hits_wide(far_owner[...] * leaves + to_column(far_slot[...]), peers * leaves)
    for n in range(rhs):
        table = everything[:, n].reshape(peers * leaves, width)
        picked[n] = dot(ids_wide, table).astype(BF16)
    far_pass(picked, v, u, terms, 0, groups)

    arrived(got_spill, send_4, recv_4, preceding)
    acc[:REACH] += jnp.where(me == 0, 0.0, got_spill[...])
    total = merged(0)
    for d in range(1, zs):
        arrived(got_z.at[d], send_3.at[d], recv_3.at[d], column[d - 1])
        total = total + got_z[d].astype(F32)
    rows_tall = hits_tall(far_row[...], leaves)
    for n in range(rhs):
        out[:, n, :] = acc[:leaves, n, :] + total[n] + scatter_rows(rows_tall, terms[n])
    for copy in sent:
        copy.wait_send()


def local(panels, diag_blocks, near_blocks, near_offsets, far_u, far_v, far_row, far_owner, far_slot):
    leaves, rhs, width = panels.shape
    pairs = far_row.shape[0]
    peers = lax.axis_size("row")
    ys = 2 if peers == 16 else 1
    zs = peers // (2 * ys)
    vmem, anywhere = (pl.BlockSpec(memory_space=m) for m in (pltpu.VMEM, pl.ANY))
    block = (rhs, leaves, width)
    sem = pltpu.SemaphoreType.DMA
    return pl.pallas_call(
        functools.partial(kernel, (zs, ys)),
        out_shape=jax.ShapeDtypeStruct(panels.shape, F32),
        in_specs=[
            vmem, anywhere, anywhere, pl.BlockSpec(memory_space=pltpu.SMEM),
            anywhere, anywhere, vmem, vmem, vmem,
        ],
        out_specs=vmem,
        scratch_shapes=[
            pltpu.VMEM(far_u.shape, BF16),
            pltpu.VMEM(far_v.shape, BF16),
            pltpu.VMEM(diag_blocks.shape, BF16),
            pltpu.VMEM(near_blocks.shape, BF16),
            pltpu.VMEM((leaves + REACH, rhs, width), F32),
            pltpu.VMEM((leaves + REACH, rhs, width), F32),
            pltpu.VMEM((rhs, pairs, width), BF16),
            pltpu.VMEM((rhs, pairs, width), F32),
            pltpu.VMEM((peers,) + block, BF16),
            pltpu.VMEM((peers // 2, 2) + block, BF16),
            pltpu.VMEM((zs, ys) + block, BF16),
            pltpu.VMEM((zs,) + block, BF16),
            pltpu.VMEM((zs,) + block, BF16),
            pltpu.VMEM((zs,) + block, BF16),
            pltpu.VMEM((zs,) + block, BF16),
            pltpu.VMEM((REACH, rhs, width), F32),
            pltpu.VMEM((REACH, rhs, width), F32),
            sem((4,)),
            sem((zs,)), sem((zs,)), sem((zs,)), sem((zs,)), sem((ys, zs)), sem((ys, zs)),
            sem((zs,)), sem((zs,)), sem((zs,)), sem((zs,)), sem((zs,)), sem((zs,)),
            sem, sem,
        ],
        compiler_params=pltpu.CompilerParams(
            vmem_limit_bytes=56 << 20, collective_id=0, has_side_effects=True
        ),
    )(
        panels, diag_blocks, near_blocks, near_offsets, far_u, far_v,
        far_row.reshape(1, pairs), far_owner, far_slot.reshape(1, pairs),
    )


def solution(mesh):
    split_all = ("groups", "row")
    return jax.shard_map(
        local,
        mesh=mesh,
        in_specs=tuple(P(split_all) for _ in range(9)),
        out_specs=P(split_all),
        check_vma=False,
    )
```

```python
import functools

import jax
import jax.numpy as jnp
from jax import lax
from jax.experimental import pallas as pl
from jax.experimental.pallas import tpu as pltpu
from jax.sharding import PartitionSpec as P

REACH = 4
GROUP = 16
F32, BF16 = jnp.float32, jnp.bfloat16


def dot(a, b):
    return lax.dot_general(a, b, (((1,), (0,)), ((), ())), preferred_element_type=F32)


def dot_t(a, b):
    return lax.dot_general(a, b, (((1,), (1,)), ((), ())), preferred_element_type=F32)


def eye(count):
    return lax.broadcasted_iota(jnp.int32, (count, count), 0) == lax.broadcasted_iota(
        jnp.int32, (count, count), 1
    )


def to_column(row):
    return jnp.sum(jnp.where(eye(row.shape[1]), row, 0), axis=1, keepdims=True)


def hits_wide(column, count):
    shape = (column.shape[0], count)
    return (column == lax.broadcasted_iota(jnp.int32, shape, 1)).astype(F32).astype(BF16)


def hits_tall(row, count):
    shape = (count, row.shape[1])
    return (row == lax.broadcasted_iota(jnp.int32, shape, 0)).astype(F32).astype(BF16)


def split(value):
    high = value.astype(BF16)
    return high, (value - high.astype(F32)).astype(BF16)


def scatter_rows(places, value):
    high, low = split(value)
    return dot(places, high) + dot(places, low)


def far_pass(picked, first, second, terms, begin, end):
    rhs, pairs, width = picked.shape
    rank = first.shape[1]
    rows, lanes = rhs * GROUP, GROUP * rank
    row_pair = lax.broadcasted_iota(jnp.int32, (rows, lanes), 0) % GROUP
    lane_pair = lax.broadcasted_iota(jnp.int32, (rows, lanes), 1) // rank
    block = (row_pair == lane_pair).astype(F32).astype(BF16)

    def step(t, carry):
        here = pl.ds(pl.multiple_of(t * GROUP, GROUP), GROUP)
        left = picked[:, here, :].reshape(rows, width)
        one = first[here].reshape(lanes, width)
        two = second[here].reshape(lanes, width)
        inner = dot_t(left, one).astype(BF16) * block
        terms[:, here, :] = dot(inner, two).reshape(rhs, GROUP, width)
        return carry

    lax.fori_loop(begin, end, step, 0, unroll=6)


def near_terms(i, leaf_x, near_x, diag, near, off, acc):
    x = leaf_x.astype(BF16)
    acc[i] += dot(x, diag[i])
    for k in range(near.shape[1]):
        acc[i] += dot_t(near_x(i + off[k, i]).astype(BF16), near[i, k])
        back = dot(x, near[i, k])
        for d in range(1, REACH + 1):
            acc[i + d] += jnp.where(off[k, i] == d, back, 0.0)


def kernel(
    shape, panels, diag_h, near_h, off, u_h, v_h, far_row, far_owner, far_slot,
    out, out_far,
    u, v, diag, near, x32, acc, picked, terms, everything, sums,
    got_core, pass_y, got_y, pass_z, got_z, spill, got_spill,
    load_sem, send_z, recv_z, send_y, recv_y, send_c, recv_c,
    send_1, recv_1, send_2, recv_2, send_3, recv_3, send_4, recv_4,
):
    zs, ys = shape
    loads = [
        pltpu.make_async_copy(a, b, load_sem.at[s])
        for s, (a, b) in enumerate(((u_h, u), (v_h, v), (near_h, near), (diag_h, diag)))
    ]
    loads[0].start()
    loads[1].start()
    leaves, rhs, width = panels.shape
    peers = everything.shape[0]
    me = lax.axis_index("row")
    c = lax.rem(me, 2)
    y = lax.rem(me // 2, ys)
    z = me // (2 * ys)
    final = me == peers - 1
    following = lax.rem(me + 1, peers)
    preceding = lax.rem(me + peers - 1, peers)

    def spot(zz, yy, cc):
        return (zz * ys + yy) * 2 + cc

    def up(d):
        return lax.rem(z + d, zs)

    def down(d):
        return lax.rem(z + zs - d, zs)

    sibling = spot(z, y, 1 - c)
    beside = spot(z, 1 - y, c) if ys == 2 else None
    column = [spot(up(d), y, c) for d in range(1, zs)]
    greeted = [sibling] + ([beside] if ys == 2 else []) + column + [following, preceding]
    barrier = pltpu.get_barrier_semaphore()
    for peer in greeted:
        pl.semaphore_signal(
            barrier, inc=1, device_id={"row": peer}, device_id_type=pl.DeviceIdType.MESH
        )

    x32[:leaves] = panels[...].astype(F32)
    x32[leaves:] = jnp.zeros((REACH, rhs, width), F32)
    acc[...] = jnp.zeros_like(acc)
    for n in range(rhs):
        everything[me, n] = x32[:leaves, n, :].astype(BF16)
    pl.semaphore_wait(barrier, len(greeted))

    sent = []

    def send(source, target, send_sem, recv_sem, peer):
        copy = pltpu.make_async_remote_copy(
            src_ref=source, dst_ref=target, send_sem=send_sem, recv_sem=recv_sem,
            device_id={"row": peer}, device_id_type=pl.DeviceIdType.MESH,
        )
        copy.start()
        sent.append(copy)

    def arrived(target, send_sem, recv_sem, peer):
        pltpu.make_async_remote_copy(
            src_ref=target, dst_ref=target, send_sem=send_sem, recv_sem=recv_sem,
            device_id={"row": peer}, device_id_type=pl.DeviceIdType.MESH,
        ).wait_recv()

    def share(owner, peer, send_sem, recv_sem):
        send(everything.at[owner], everything.at[owner], send_sem, recv_sem, peer)

    def settled(owner, send_sem, recv_sem):
        arrived(everything.at[owner], send_sem, recv_sem, sibling)

    far_first = list(range(zs - 1, 0, -1))
    for d in far_first:
        share(me, column[d - 1], send_z.at[d], recv_z.at[d])
    if ys == 2:
        share(me, beside, send_y.at[0], recv_y.at[0])
    share(me, sibling, send_c.at[0, 0], recv_c.at[0, 0])

    ids = far_owner[...] * leaves + far_slot[...]
    places = hits_tall(ids, peers * leaves)
    rows_wide = hits_wide(to_column(far_row[...]), leaves)
    for n in range(rhs):
        picked[n] = dot(rows_wide, x32[:leaves, n, :].astype(BF16)).astype(BF16)
    loads[0].wait()
    loads[1].wait()
    loads[2].start()
    loads[3].start()
    groups = far_row.shape[1] // GROUP
    far_pass(picked, u, v, terms, 0, groups // 2)
    for d in range(1, zs):
        owner = spot(down(d), y, c)
        settled(owner, send_z.at[d], recv_z.at[d])
        if ys == 2:
            share(owner, beside, send_y.at[d], recv_y.at[d])
        share(owner, sibling, send_c.at[0, d], recv_c.at[0, d])
    far_pass(picked, u, v, terms, groups // 2, groups)
    for n in range(rhs):
        sums[:, :, n] = scatter_rows(places, terms[n]).astype(BF16).reshape(
            peers // 2, 2, leaves, width
        )

    order = far_first + [0]
    for d in order:
        send(
            sums.at[pl.ds(up(d) * ys, ys), 1 - c], got_core.at[d],
            send_1.at[d], recv_1.at[d], sibling,
        )
    if ys == 2:
        for d in range(zs):
            owner = spot(down(d), 1 - y, c)
            settled(owner, send_y.at[d], recv_y.at[d])
            share(owner, sibling, send_c.at[1, d], recv_c.at[1, d])

    loads[2].wait()
    loads[3].wait()

    def step(i, carry):
        near_terms(i, x32[i], lambda j: x32[j], diag, near, off, acc)
        return carry

    def joined(d, yy):
        return sums[up(d) * ys + yy, c].astype(F32) + got_core[d, yy].astype(F32)

    lax.fori_loop(0, 2, step, 0, unroll=2)
    for d in order:
        arrived(got_core.at[d], send_1.at[d], recv_1.at[d], sibling)
        if ys == 2:
            pass_y[d] = joined(d, 1 - y).astype(BF16)
            send(pass_y.at[d], got_y.at[d], send_2.at[d], recv_2.at[d], beside)
    lax.fori_loop(2, 8, step, 0, unroll=3)

    def merged(d):
        value = joined(d, y)
        if ys == 2:
            arrived(got_y.at[d], send_2.at[d], recv_2.at[d], beside)
            value = value + got_y[d].astype(F32)
        return value

    for d in far_first:
        pass_z[d] = merged(d).astype(BF16)
        send(pass_z.at[d], got_z.at[d], send_3.at[d], recv_3.at[d], column[d - 1])
    lax.fori_loop(8, leaves - REACH, step, 0, unroll=4)

    for part in range(ys):
        for d in range(zs):
            owner = spot(down(d), y if part == 0 else 1 - y, 1 - c)
            settled(owner, send_c.at[part, d], recv_c.at[part, d])
    for n in range(rhs):
        ahead = everything[following, n].astype(F32)[:REACH]
        x32[leaves:, n, :] = jnp.where(final, 0.0, ahead)
    lax.fori_loop(leaves - REACH, leaves, step, 0, unroll=4)
    spill[...] = acc[leaves:]
    send(spill, got_spill, send_4, recv_4, following)

    ids_wide = hits_wide(to_column(ids), peers * leaves)
    for n in range(rhs):
        table = everything[:, n].reshape(peers * leaves, width)
        picked[n] = dot(ids_wide, table).astype(BF16)
    far_pass(picked, v, u, terms, 0, groups)

    arrived(got_spill, send_4, recv_4, preceding)
    acc[:REACH] += jnp.where(me == 0, 0.0, got_spill[...])
    total = merged(0)
    for d in range(1, zs):
        arrived(got_z.at[d], send_3.at[d], recv_3.at[d], column[d - 1])
        total = total + got_z[d].astype(F32)
    rows_tall = hits_tall(far_row[...], leaves)
    for n in range(rhs):
        out[:, n, :] = acc[:leaves, n, :] + scatter_rows(rows_tall, terms[n])
        out_far[:, n, :] = total[n]
    for copy in sent:
        copy.wait_send()


def local(panels, diag_blocks, near_blocks, near_offsets, far_u, far_v, far_row, far_owner, far_slot):
    leaves, rhs, width = panels.shape
    pairs = far_row.shape[0]
    peers = lax.axis_size("row")
    ys = 2 if peers == 16 else 1
    zs = peers // (2 * ys)
    vmem, anywhere = (pl.BlockSpec(memory_space=m) for m in (pltpu.VMEM, pl.ANY))
    block = (rhs, leaves, width)
    sem = pltpu.SemaphoreType.DMA
    near_part, far_part = pl.pallas_call(
        functools.partial(kernel, (zs, ys)),
        out_shape=(jax.ShapeDtypeStruct(panels.shape, F32),) * 2,
        in_specs=[
            vmem, anywhere, anywhere, pl.BlockSpec(memory_space=pltpu.SMEM),
            anywhere, anywhere, vmem, vmem, vmem,
        ],
        out_specs=(vmem, vmem),
        scratch_shapes=[
            pltpu.VMEM(far_u.shape, BF16),
            pltpu.VMEM(far_v.shape, BF16),
            pltpu.VMEM(diag_blocks.shape, BF16),
            pltpu.VMEM(near_blocks.shape, BF16),
            pltpu.VMEM((leaves + REACH, rhs, width), F32),
            pltpu.VMEM((leaves + REACH, rhs, width), F32),
            pltpu.VMEM((rhs, pairs, width), BF16),
            pltpu.VMEM((rhs, pairs, width), F32),
            pltpu.VMEM((peers,) + block, BF16),
            pltpu.VMEM((peers // 2, 2) + block, BF16),
            pltpu.VMEM((zs, ys) + block, BF16),
            pltpu.VMEM((zs,) + block, BF16),
            pltpu.VMEM((zs,) + block, BF16),
            pltpu.VMEM((zs,) + block, BF16),
            pltpu.VMEM((zs,) + block, BF16),
            pltpu.VMEM((REACH, rhs, width), F32),
            pltpu.VMEM((REACH, rhs, width), F32),
            sem((4,)),
            sem((zs,)), sem((zs,)), sem((zs,)), sem((zs,)), sem((ys, zs)), sem((ys, zs)),
            sem((zs,)), sem((zs,)), sem((zs,)), sem((zs,)), sem((zs,)), sem((zs,)),
            sem, sem,
        ],
        compiler_params=pltpu.CompilerParams(
            vmem_limit_bytes=56 << 20, collective_id=0, has_side_effects=True
        ),
    )(
        panels, diag_blocks, near_blocks, near_offsets.T, far_u, far_v,
        far_row.reshape(1, pairs), far_owner.T, far_slot.reshape(1, pairs),
    )
    return near_part + far_part


def solution(mesh):
    split_all = ("groups", "row")
    return jax.shard_map(
        local,
        mesh=mesh,
        in_specs=tuple(P(split_all) for _ in range(9)),
        out_specs=P(split_all),
        check_vma=False,
    )
```

```python
import functools

import jax
import jax.numpy as jnp
from jax import lax
from jax.experimental import pallas as pl
from jax.experimental.pallas import tpu as pltpu
from jax.sharding import PartitionSpec as P

REACH = 4
GROUP = 16
F32, BF16 = jnp.float32, jnp.bfloat16


def dot(a, b):
    return lax.dot_general(a, b, (((1,), (0,)), ((), ())), preferred_element_type=F32)


def dot_t(a, b):
    return lax.dot_general(a, b, (((1,), (1,)), ((), ())), preferred_element_type=F32)


def eye(count):
    return lax.broadcasted_iota(jnp.int32, (count, count), 0) == lax.broadcasted_iota(
        jnp.int32, (count, count), 1
    )


def to_column(row):
    return jnp.sum(jnp.where(eye(row.shape[1]), row, 0), axis=1, keepdims=True)


def hits_wide(column, count):
    shape = (column.shape[0], count)
    return (column == lax.broadcasted_iota(jnp.int32, shape, 1)).astype(F32).astype(BF16)


def hits_tall(row, count):
    shape = (count, row.shape[1])
    return (row == lax.broadcasted_iota(jnp.int32, shape, 0)).astype(F32).astype(BF16)


def split(value):
    high = value.astype(BF16)
    return high, (value - high.astype(F32)).astype(BF16)


def scatter_rows(places, value):
    high, low = split(value)
    return dot(places, high) + dot(places, low)


def far_pass(picked, first, second, terms, begin, end):
    rhs, pairs, width = picked.shape
    rank = first.shape[1]
    rows, lanes = rhs * GROUP, GROUP * rank
    row_pair = lax.broadcasted_iota(jnp.int32, (rows, lanes), 0) % GROUP
    lane_pair = lax.broadcasted_iota(jnp.int32, (rows, lanes), 1) // rank
    block = (row_pair == lane_pair).astype(F32).astype(BF16)

    def step(t, carry):
        here = pl.ds(pl.multiple_of(t * GROUP, GROUP), GROUP)
        left = picked[:, here, :].reshape(rows, width)
        one = first[here].reshape(lanes, width)
        two = second[here].reshape(lanes, width)
        inner = dot_t(left, one).astype(BF16) * block
        terms[:, here, :] = dot(inner, two).reshape(rhs, GROUP, width)
        return carry

    lax.fori_loop(begin, end, step, 0, unroll=6)


def near_terms(i, leaf_x, near_x, diag, near, off, acc):
    x = leaf_x.astype(BF16)
    acc[i] += dot(x, diag[i])
    for k in range(near.shape[1]):
        acc[i] += dot_t(near_x(i + off[k, i]).astype(BF16), near[i, k])
        back = dot(x, near[i, k])
        for d in range(1, REACH + 1):
            acc[i + d] += jnp.where(off[k, i] == d, back, 0.0)


def kernel(
    shape, panels, diag_h, near_h, off, u_h, v_h, far_row, far_owner, far_slot,
    out, out_far,
    u, v, diag, near, x32, acc, picked, terms, everything, sums,
    got_core, pass_y, got_y, pass_z, got_z, spill, got_spill,
    load_sem, send_z, recv_z, send_y, recv_y, send_c, recv_c,
    send_1, recv_1, send_2, recv_2, send_3, recv_3, send_4, recv_4,
):
    zs, ys = shape
    loads = [
        pltpu.make_async_copy(a, b, load_sem.at[s])
        for s, (a, b) in enumerate(((u_h, u), (v_h, v), (near_h, near), (diag_h, diag)))
    ]
    loads[0].start()
    loads[1].start()
    leaves, rhs, width = panels.shape
    peers = everything.shape[0]
    me = lax.axis_index("row")
    c = lax.rem(me, 2)
    y = lax.rem(me // 2, ys)
    z = me // (2 * ys)
    final = me == peers - 1
    following = lax.rem(me + 1, peers)
    preceding = lax.rem(me + peers - 1, peers)

    def spot(zz, yy, cc):
        return (zz * ys + yy) * 2 + cc

    def up(d):
        return lax.rem(z + d, zs)

    def down(d):
        return lax.rem(z + zs - d, zs)

    sibling = spot(z, y, 1 - c)
    beside = spot(z, 1 - y, c) if ys == 2 else None
    column = [spot(up(d), y, c) for d in range(1, zs)]
    greeted = [sibling] + ([beside] if ys == 2 else []) + column + [following, preceding]
    barrier = pltpu.get_barrier_semaphore()
    for peer in greeted:
        pl.semaphore_signal(
            barrier, inc=1, device_id={"row": peer}, device_id_type=pl.DeviceIdType.MESH
        )

    x32[:leaves] = panels[...].astype(F32)
    x32[leaves:] = jnp.zeros((REACH, rhs, width), F32)
    acc[...] = jnp.zeros_like(acc)
    for n in range(rhs):
        everything[me, n] = x32[:leaves, n, :].astype(BF16)
    pl.semaphore_wait(barrier, len(greeted))

    sent = []

    def send(source, target, send_sem, recv_sem, peer):
        copy = pltpu.make_async_remote_copy(
            src_ref=source, dst_ref=target, send_sem=send_sem, recv_sem=recv_sem,
            device_id={"row": peer}, device_id_type=pl.DeviceIdType.MESH,
        )
        copy.start()
        sent.append(copy)

    def arrived(target, send_sem, recv_sem, peer):
        pltpu.make_async_remote_copy(
            src_ref=target, dst_ref=target, send_sem=send_sem, recv_sem=recv_sem,
            device_id={"row": peer}, device_id_type=pl.DeviceIdType.MESH,
        ).wait_recv()

    def share(owner, peer, send_sem, recv_sem):
        send(everything.at[owner], everything.at[owner], send_sem, recv_sem, peer)

    def settled(owner, send_sem, recv_sem):
        arrived(everything.at[owner], send_sem, recv_sem, sibling)

    far_first = list(range(zs - 1, 0, -1))
    for d in far_first:
        share(me, column[d - 1], send_z.at[d], recv_z.at[d])
    if ys == 2:
        share(me, beside, send_y.at[0], recv_y.at[0])
    share(me, sibling, send_c.at[0, 0], recv_c.at[0, 0])

    ids = far_owner[...] * leaves + far_slot[...]
    places = hits_tall(ids, peers * leaves)
    rows_wide = hits_wide(to_column(far_row[...]), leaves)
    for n in range(rhs):
        picked[n] = dot(rows_wide, x32[:leaves, n, :].astype(BF16)).astype(BF16)
    loads[0].wait()
    loads[1].wait()
    loads[2].start()
    loads[3].start()
    groups = far_row.shape[1] // GROUP
    far_pass(picked, u, v, terms, 0, groups)
    for n in range(rhs):
        sums[:, :, n] = scatter_rows(places, terms[n]).astype(BF16).reshape(
            peers // 2, 2, leaves, width
        )

    order = far_first + [0]
    for d in order:
        send(
            sums.at[pl.ds(up(d) * ys, ys), 1 - c], got_core.at[d],
            send_1.at[d], recv_1.at[d], sibling,
        )
    for d in range(1, zs):
        owner = spot(down(d), y, c)
        settled(owner, send_z.at[d], recv_z.at[d])
        if ys == 2:
            share(owner, beside, send_y.at[d], recv_y.at[d])
        share(owner, sibling, send_c.at[0, d], recv_c.at[0, d])

    loads[2].wait()
    loads[3].wait()

    def step(i, carry):
        near_terms(i, x32[i], lambda j: x32[j], diag, near, off, acc)
        return carry

    def joined(d, yy):
        return sums[up(d) * ys + yy, c].astype(F32) + got_core[d, yy].astype(F32)

    lax.fori_loop(0, 2, step, 0, unroll=2)
    for d in order:
        arrived(got_core.at[d], send_1.at[d], recv_1.at[d], sibling)
        if ys == 2:
            pass_y[d] = joined(d, 1 - y).astype(BF16)
            send(pass_y.at[d], got_y.at[d], send_2.at[d], recv_2.at[d], beside)
    lax.fori_loop(2, 8, step, 0, unroll=3)
    if ys == 2:
        for d in range(zs):
            owner = spot(down(d), 1 - y, c)
            settled(owner, send_y.at[d], recv_y.at[d])
            share(owner, sibling, send_c.at[1, d], recv_c.at[1, d])


    def merged(d):
        value = joined(d, y)
        if ys == 2:
            arrived(got_y.at[d], send_2.at[d], recv_2.at[d], beside)
            value = value + got_y[d].astype(F32)
        return value

    for d in far_first:
        pass_z[d] = merged(d).astype(BF16)
        send(pass_z.at[d], got_z.at[d], send_3.at[d], recv_3.at[d], column[d - 1])
    lax.fori_loop(8, leaves - REACH, step, 0, unroll=4)

    for part in range(ys):
        for d in range(zs):
            owner = spot(down(d), y if part == 0 else 1 - y, 1 - c)
            settled(owner, send_c.at[part, d], recv_c.at[part, d])
    for n in range(rhs):
        ahead = everything[following, n].astype(F32)[:REACH]
        x32[leaves:, n, :] = jnp.where(final, 0.0, ahead)
    lax.fori_loop(leaves - REACH, leaves, step, 0, unroll=4)
    spill[...] = acc[leaves:]
    send(spill, got_spill, send_4, recv_4, following)

    ids_wide = hits_wide(to_column(ids), peers * leaves)
    for n in range(rhs):
        table = everything[:, n].reshape(peers * leaves, width)
        picked[n] = dot(ids_wide, table).astype(BF16)
    far_pass(picked, v, u, terms, 0, groups)

    arrived(got_spill, send_4, recv_4, preceding)
    acc[:REACH] += jnp.where(me == 0, 0.0, got_spill[...])
    total = merged(0)
    for d in range(1, zs):
        arrived(got_z.at[d], send_3.at[d], recv_3.at[d], column[d - 1])
        total = total + got_z[d].astype(F32)
    rows_tall = hits_tall(far_row[...], leaves)
    for n in range(rhs):
        out[:, n, :] = acc[:leaves, n, :] + scatter_rows(rows_tall, terms[n])
        out_far[:, n, :] = total[n]
    for copy in sent:
        copy.wait_send()


def local(panels, diag_blocks, near_blocks, near_offsets, far_u, far_v, far_row, far_owner, far_slot):
    leaves, rhs, width = panels.shape
    pairs = far_row.shape[0]
    peers = lax.axis_size("row")
    ys = 2 if peers == 16 else 1
    zs = peers // (2 * ys)
    vmem, anywhere = (pl.BlockSpec(memory_space=m) for m in (pltpu.VMEM, pl.ANY))
    block = (rhs, leaves, width)
    sem = pltpu.SemaphoreType.DMA
    near_part, far_part = pl.pallas_call(
        functools.partial(kernel, (zs, ys)),
        out_shape=(jax.ShapeDtypeStruct(panels.shape, F32),) * 2,
        in_specs=[
            vmem, anywhere, anywhere, pl.BlockSpec(memory_space=pltpu.SMEM),
            anywhere, anywhere, vmem, vmem, vmem,
        ],
        out_specs=(vmem, vmem),
        scratch_shapes=[
            pltpu.VMEM(far_u.shape, BF16),
            pltpu.VMEM(far_v.shape, BF16),
            pltpu.VMEM(diag_blocks.shape, BF16),
            pltpu.VMEM(near_blocks.shape, BF16),
            pltpu.VMEM((leaves + REACH, rhs, width), F32),
            pltpu.VMEM((leaves + REACH, rhs, width), F32),
            pltpu.VMEM((rhs, pairs, width), BF16),
            pltpu.VMEM((rhs, pairs, width), F32),
            pltpu.VMEM((peers,) + block, BF16),
            pltpu.VMEM((peers // 2, 2) + block, BF16),
            pltpu.VMEM((zs, ys) + block, BF16),
            pltpu.VMEM((zs,) + block, BF16),
            pltpu.VMEM((zs,) + block, BF16),
            pltpu.VMEM((zs,) + block, BF16),
            pltpu.VMEM((zs,) + block, BF16),
            pltpu.VMEM((REACH, rhs, width), F32),
            pltpu.VMEM((REACH, rhs, width), F32),
            sem((4,)),
            sem((zs,)), sem((zs,)), sem((zs,)), sem((zs,)), sem((ys, zs)), sem((ys, zs)),
            sem((zs,)), sem((zs,)), sem((zs,)), sem((zs,)), sem((zs,)), sem((zs,)),
            sem, sem,
        ],
        compiler_params=pltpu.CompilerParams(
            vmem_limit_bytes=56 << 20, collective_id=0, has_side_effects=True
        ),
    )(
        panels, diag_blocks, near_blocks, near_offsets.T, far_u, far_v,
        far_row.reshape(1, pairs), far_owner.T, far_slot.reshape(1, pairs),
    )
    return near_part + far_part


def solution(mesh):
    split_all = ("groups", "row")
    return jax.shard_map(
        local,
        mesh=mesh,
        in_specs=tuple(P(split_all) for _ in range(9)),
        out_specs=P(split_all),
        check_vma=False,
    )
```
